32 devices in a mesh: dp: 8 (over z, x), tensor: 4 (over y, core).
Axes of the slice: x: 2, y: 2, z: 4, core: 2. Of those that a mesh axis runs over, the one named last changes fastest.
Arguments:
- activations: bfloat16 [4096, 5120], P('dp', 'tensor'), may hold values from -6 to 6
- out_grad: bfloat16 [4096, 5120], P('dp', 'tensor'), may hold values from -6 to 6
- gate_pre: bfloat16 [4096, 14336], P('dp', 'tensor'), may hold values from -6 to 6
- up_pre: bfloat16 [4096, 14336], P('dp', 'tensor'), may hold values from -6 to 6
- down_weight: bfloat16 [14336, 5120], P(('tensor', 'dp')), may hold values from -0.046875 to 0.046875
- proj_model: bfloat16 [5120, 64], replicated, may hold values from -0.078125 to 0.078125
- proj_hidden: bfloat16 [14336, 64], P('tensor'), may hold values from -0.046875 to 0.046875
- lengths: int32 [32], P('dp'), may hold values from 1 to 128, as said below
Outputs:
- grad_gate: bfloat16 [4096, 14336], P('dp', 'tensor')
- grad_up: bfloat16 [4096, 14336], P('dp', 'tensor')
- features: float32 [32, 3, 4096], P('dp')
The draws below stay inside these ranges and needn't reach their ends.
Inputs may be any that keep to these rules, and one draw needn't show every extreme that they name: In every block of 4 slots of one index of dp the lengths sum to at most 512. In every draw one slot among all 32 has exactly 128 tokens and another exactly 1.
All inputs are finite; a program needn't handle non-finite values.
Results may differ from the reference program's by a relative error of at most 0.003.
Values may be sent and summed in bfloat16 or wider, within the bound.
A program may use at most 128 MiB of HBM per device.

```python
import jax
import jax.numpy as jnp
from jax import lax

D = 5120
FFW = 14336
RANK = 64
TOK_DEV = 512
E_DEV = 4
TOKENS = 4096
EXAMPLES = 32
N_DP = 8


def draw_lengths(key, part):
    longest = TOK_DEV // E_DEV
    values = jax.random.randint(key, (EXAMPLES,), 1, longest + 1).astype(jnp.int32)
    top_slot = jax.random.randint(jax.random.fold_in(key, 7), (), 0, EXAMPLES).astype(jnp.int32)
    low_slot = (top_slot + 1) % EXAMPLES
    places = jnp.arange(EXAMPLES, dtype=jnp.int32)
    values = jnp.where(places == low_slot, 1, values)
    values = jnp.where(places == top_slot, longest, values)
    return values.astype(jnp.int32)


def block_scale(own_key, shape, shards, smallest, top_value):
    factor_of, own = 1.0, jax.random.fold_in(own_key, 6)
    for dim, blocks in shards:
        draws = jnp.exp(jax.random.uniform(jax.random.fold_in(own, dim), (blocks,), jnp.float32, smallest / len(shards), top_value / len(shards)))
        factor_of = factor_of * jnp.repeat(draws, shape[dim] // blocks).reshape([-1 if axis == dim else 1 for axis in range(len(shape))])
    return factor_of


def bell_draw(own_key, extent, scale, most, cuts=(), kind=jnp.bfloat16):
    array = scale * jax.random.normal(own_key, extent, jnp.float32)
    if cuts:
        array = array * block_scale(own_key, extent, cuts, -0.22, 0.18)
    return jnp.clip(array, -most, most).astype(kind)


def setup_inputs(seed: int = 0) -> dict:
    splits = jax.random.split(jax.random.key(seed), 9)
    activations = bell_draw(splits[0], (TOKENS, D), 1.0, 6.0, ((0, 8), (1, 4)))
    out_grad = bell_draw(splits[1], (TOKENS, D), 1.0, 6.0, ((0, 8), (1, 4)))
    gate_pre = bell_draw(splits[2], (TOKENS, FFW), 1.5, 6.0, ((0, 8), (1, 4)))
    up_pre = bell_draw(splits[3], (TOKENS, FFW), 1.0, 6.0, ((0, 8), (1, 4)))
    down_weight = bell_draw(splits[4], (FFW, D), FFW ** -0.5, 0.046875, ((0, 32),))
    proj_model = bell_draw(splits[5], (D, RANK), D ** -0.5, 0.078125)
    proj_hidden = bell_draw(splits[6], (FFW, RANK), FFW ** -0.5, 0.046875, ((0, 4),))
    lengths = draw_lengths(jax.random.fold_in(splits[8], 71), 0)
    return {"activations": activations, "out_grad": out_grad, "gate_pre": gate_pre, "up_pre": up_pre, "down_weight": down_weight, "proj_model": proj_model, "proj_hidden": proj_hidden, "lengths": lengths}


def block_features(args, down_weight, proj_model, proj_hidden):
    activations, out_grad, gate_pre, up_pre, lengths = args
    offsets = jnp.cumsum(lengths).astype(jnp.int32) - lengths
    rows = jnp.arange(activations.shape[0], dtype=jnp.int32)[:, None]
    member = jnp.logical_and(rows >= offsets[None, :], rows < (offsets + lengths)[None, :]).astype(jnp.float32)
    live = lax.optimization_barrier(jnp.sum(member, axis=1))
    masked = out_grad * live[:, None].astype(jnp.bfloat16)
    hidden_grad = jnp.dot(masked, down_weight.T, preferred_element_type=jnp.float32)
    gate32 = gate_pre.astype(jnp.float32)
    up32 = up_pre.astype(jnp.float32)
    sig = jax.nn.sigmoid(gate32)
    silu = gate32 * sig
    grad_up = (hidden_grad * silu).astype(jnp.bfloat16)
    grad_gate = (hidden_grad * up32 * sig * (1.0 + gate32 * (1.0 - sig))).astype(jnp.bfloat16)
    hidden = (silu * up32).astype(jnp.bfloat16)
    in_proj = jnp.dot(activations, proj_model, preferred_element_type=jnp.float32)
    hidden_proj = jnp.dot(hidden, proj_hidden, preferred_element_type=jnp.float32)
    gate_proj = jnp.dot(grad_gate, proj_hidden, preferred_element_type=jnp.float32)
    up_proj = jnp.dot(grad_up, proj_hidden, preferred_element_type=jnp.float32)
    out_proj = jnp.dot(masked, proj_model, preferred_element_type=jnp.float32)
    weight = member / jnp.sqrt(lengths.astype(jnp.float32))[None, :]

    def pair(left, right):
        mats = jnp.einsum('te,ti,tj->eij', weight, left, right, precision=lax.Precision.HIGHEST)
        return mats.reshape(mats.shape[0], RANK * RANK)
    feats = jnp.stack([pair(in_proj, gate_proj), pair(in_proj, up_proj), pair(hidden_proj, out_proj)], axis=1)
    return (grad_gate, grad_up, feats)

def reference(activations, out_grad, gate_pre, up_pre, down_weight, proj_model, proj_hidden, lengths):
    blocks = (activations.reshape(N_DP, TOK_DEV, D), out_grad.reshape(N_DP, TOK_DEV, D), gate_pre.reshape(N_DP, TOK_DEV, FFW), up_pre.reshape(N_DP, TOK_DEV, FFW), lengths.reshape(N_DP, E_DEV))
    grad_gate, grad_up, feats = lax.map(lambda a: block_features(a, down_weight, proj_model, proj_hidden), blocks)
    return (grad_gate.reshape(TOKENS, FFW), grad_up.reshape(TOKENS, FFW), feats.reshape(EXAMPLES, 3, RANK * RANK))
```

```python
import functools

import jax
import jax.numpy as jnp
from jax import lax
from jax.experimental import pallas as pl
from jax.experimental.pallas import tpu as pltpu
from jax.sharding import PartitionSpec as P

MESH = pl.DeviceIdType.MESH
LEVELS = 32767.0


def plan(mesh):
    n_dp, n_tensor = mesh.shape["dp"], mesh.shape["tensor"]
    nz = 4 if n_dp % 4 == 0 else n_dp
    nc = 2 if n_tensor % 2 == 0 else 1
    return nz, n_dp // nz, n_tensor // nc, nc


def grad_kernel(
    nz, nx, ny, nc, tok_in, w_in, q_out, sc_out,
    tok, w, qs, scs,
    loc, zs, zr, ys, yr, cs, cr, xs, xr, rs, rr, ss, sr,
):
    dp = lax.axis_index("dp")
    tn = lax.axis_index("tensor")
    z, x = lax.div(dp, nx), lax.rem(dp, nx)
    y, c = lax.div(tn, nc), lax.rem(tn, nc)
    width = tok.shape[3]
    n_t = ny * nc

    def at_z(zz):
        return (zz * nx + x, tn)

    def at_x(k):
        return (z * nx + lax.rem(x + k, nx), tn)

    def at_y(k):
        return (dp, lax.rem(y + k, ny) * nc + c)

    def at_c(k):
        return (dp, y * nc + lax.rem(c + k, nc))

    barrier = pltpu.get_barrier_semaphore()
    peers = [at_z(lax.rem(z + k, nz)) for k in range(1, nz)]
    peers += [at_x(k) for k in range(1, nx)]
    peers += [at_y(k) for k in range(1, ny)]
    peers += [at_c(k) for k in range(1, nc)]
    own_tok = pltpu.make_async_copy(tok_in, tok.at[z, tn], loc.at[0])
    own_tok.start()
    own_w = pltpu.make_async_copy(w_in, w.at[x], loc.at[1])
    own_w.start()
    for peer in peers:
        pl.semaphore_signal(barrier, inc=1, device_id=peer, device_id_type=MESH)
    pl.semaphore_wait(barrier, len(peers))

    def remote(src, dst, send, recv, device):
        return pltpu.make_async_remote_copy(
            src_ref=src, dst_ref=dst, send_sem=send, recv_sem=recv,
            device_id=device, device_id_type=MESH,
        )

    def w_copy(k):
        return remote(w_in, w.at[x], xs.at[k - 1], xr.at[x], at_x(k))

    def z_copy(b, side):
        target = z + 1 if side else z - 1
        return remote(tok.at[b, tn], tok.at[b, tn], zs.at[b, side], zr.at[b], at_z(target))

    def y_copy(b, k):
        return remote(tok.at[b, tn], tok.at[b, tn], ys.at[b, k - 1], yr.at[b, k - 1], at_y(k))

    def c_copy(b, k, kc):
        t = lax.rem(y - k + ny, ny) * nc + c
        return remote(tok.at[b, t], tok.at[b, t], cs.at[b, k, kc - 1], cr.at[b, k, kc - 1], at_c(kc))

    def q_copy(b, xi):
        return remote(qs.at[b, xi], q_out.at[z, xi], rs.at[b, xi], rr.at[z, xi], at_z(b))

    def sc_copy(b, xi):
        return remote(scs.at[b, xi], sc_out.at[z, xi], ss.at[b, xi], sr.at[z, xi], at_z(b))

    def q_own(xi):
        return pltpu.make_async_copy(qs.at[z, xi], q_out.at[z, xi], rs.at[z, xi])

    def sc_own(xi):
        return pltpu.make_async_copy(scs.at[z, xi], sc_out.at[z, xi], ss.at[z, xi])

    near = jnp.minimum(z, nz - 1 - z)

    def block_of(i):
        half = lax.div(i + 1, 2)
        both = jnp.where(lax.rem(i, 2) == 1, z - half, z + half)
        tail = jnp.where(z == near, i, nz - 1 - i)
        return jnp.where(i <= 2 * near, both, tail)

    def goes_right(b):
        return jnp.logical_and(b <= z, z < nz - 1)

    def goes_left(b):
        return jnp.logical_and(b >= z, z > 0)

    def spread(b):
        pl.when(goes_right(b))(lambda: z_copy(b, 1).start())
        pl.when(goes_left(b))(lambda: z_copy(b, 0).start())
        for k in range(1, ny):
            y_copy(b, k).start()
        for kc in range(1, nc):
            c_copy(b, 0, kc).start()

    def complete(b):
        for k in range(1, ny):
            y_copy(b, k).wait_recv()
            for kc in range(1, nc):
                c_copy(b, k, kc).start()
        for k in range(ny):
            for kc in range(1, nc):
                c_copy(b, k, kc).wait_recv()

    def product(b, xi):
        total = None
        for t in range(n_t):
            part = lax.dot_general(
                tok[b, t], w[xi, :, t * width:(t + 1) * width],
                (((1,), (1,)), ((), ())), preferred_element_type=jnp.float32,
            )
            total = part if total is None else total + part
        top = jnp.maximum(jnp.max(jnp.abs(total), axis=0, keepdims=True), 1e-30)
        qs[b, xi] = jnp.round(total * (LEVELS / top)).astype(jnp.int32).astype(jnp.int16)
        scs[b, xi] = jnp.broadcast_to(top * (1.0 / LEVELS), scs.shape[2:])

        @pl.when(b == z)
        def _():
            q_own(xi).start()
            sc_own(xi).start()

        @pl.when(b != z)
        def _():
            q_copy(b, xi).start()
            sc_copy(b, xi).start()

    own_tok.wait()
    spread(z)
    for k in range(1, nx):
        w_copy(k).start()
    own_w.wait()

    @pl.loop(1, nz + 1)
    def _(i):
        @pl.when(i < nz)
        def _():
            b = block_of(i)
            z_copy(b, 0).wait_recv()
            spread(b)

        b = block_of(i - 1)
        complete(b)
        product(b, x)

    for k in range(1, nx):
        xi = lax.rem(x - k + nx, nx)
        remote(w_in, w.at[xi], xs.at[k - 1], xr.at[xi], at_x(k)).wait_recv()

        @pl.loop(0, nz)
        def _(i):
            product(block_of(lax.rem(i + 1, nz)), xi)

    for k in range(1, nx):
        w_copy(k).wait_send()

    @pl.loop(0, nz)
    def _(b):
        pl.when(goes_right(b))(lambda: z_copy(b, 1).wait_send())
        pl.when(goes_left(b))(lambda: z_copy(b, 0).wait_send())
        for k in range(1, ny):
            y_copy(b, k).wait_send()
        for k in range(ny):
            for kc in range(1, nc):
                c_copy(b, k, kc).wait_send()
        for xi in range(nx):
            @pl.when(b == z)
            def _():
                q_own(xi).wait()
                sc_own(xi).wait()

            @pl.when(b != z)
            def _():
                q_copy(b, xi).wait_send()
                sc_copy(b, xi).wait_send()
                remote(qs.at[b, xi], q_out.at[b, xi], rs.at[b, xi], rr.at[b, xi], at_z(b)).wait_recv()
                remote(scs.at[b, xi], sc_out.at[b, xi], ss.at[b, xi], sr.at[b, xi], at_z(b)).wait_recv()


def hidden_grads(sizes, masked_part, down_weight):
    nz, nx, ny, nc = sizes
    rows, width = masked_part.shape
    units, model = down_weight.shape
    n_t = ny * nc
    dma = pltpu.SemaphoreType.DMA
    any_spec = pl.BlockSpec(memory_space=pl.ANY)
    return pl.pallas_call(
        functools.partial(grad_kernel, nz, nx, ny, nc),
        out_shape=(
            jax.ShapeDtypeStruct((nz, nx, rows, units), jnp.int16),
            jax.ShapeDtypeStruct((nz, nx, 8, units), jnp.float32),
        ),
        in_specs=[any_spec, any_spec],
        out_specs=(any_spec, any_spec),
        scratch_shapes=[
            pltpu.VMEM((nz, n_t, rows, width), jnp.bfloat16),
            pltpu.VMEM((nx, units, model), jnp.bfloat16),
            pltpu.VMEM((nz, nx, rows, units), jnp.int16),
            pltpu.VMEM((nz, nx, 8, units), jnp.float32),
            dma((2,)),
            dma((nz, 2)), dma((nz,)),
            dma((nz, max(ny - 1, 1))), dma((nz, max(ny - 1, 1))),
            dma((nz, ny, max(nc - 1, 1))), dma((nz, ny, max(nc - 1, 1))),
            dma((max(nx - 1, 1),)), dma((nx,)),
            dma((nz, nx)), dma((nz, nx)),
            dma((nz, nx)), dma((nz, nx)),
        ],
        compiler_params=pltpu.CompilerParams(
            collective_id=0, has_side_effects=True, vmem_limit_bytes=56 * 2**20
        ),
        cost_estimate=pl.CostEstimate(
            flops=2 * nz * rows * nx * units * model,
            bytes_accessed=2 * (rows * width + units * model + nz * nx * rows * units),
            transcendentals=0,
        ),
        name="hidden_grads",
    )(masked_part, down_weight)


def epilogue_kernel(nz, nx, q_ref, sc_ref, gate_ref, up_ref, proj_ref, gg_ref, gu_ref, part_ref):
    rows = gate_ref.shape[0]
    units = q_ref.shape[3]
    chunk = nx * units
    total = None
    for zz in range(nz):
        cols = slice(zz * chunk, (zz + 1) * chunk)
        grad = jnp.concatenate(
            [
                q_ref[zz, xi].astype(jnp.int32).astype(jnp.float32) * sc_ref[zz, xi, 0:1, :]
                for xi in range(nx)
            ],
            axis=1,
        )
        gate32 = gate_ref[:, cols].astype(jnp.float32)
        up32 = up_ref[:, cols].astype(jnp.float32)
        sig = jax.nn.sigmoid(gate32)
        silu = gate32 * sig
        gu = (grad * silu).astype(jnp.bfloat16)
        gg = (grad * up32 * sig * (1.0 + gate32 * (1.0 - sig))).astype(jnp.bfloat16)
        hid = (silu * up32).astype(jnp.bfloat16)
        gu_ref[:, cols] = gu
        gg_ref[:, cols] = gg
        stacked = jnp.concatenate([gg, gu, hid], axis=0)
        part = jnp.dot(stacked, proj_ref[cols, :], preferred_element_type=jnp.float32)
        total = part if total is None else total + part
    for i in range(3):
        part_ref[i] = total[i * rows:(i + 1) * rows]


def epilogue(sizes, q, sc, gate_pre, up_pre, proj_hidden):
    nz, nx = sizes[:2]
    rows, hidden = gate_pre.shape
    units, rank = q.shape[3], proj_hidden.shape[1]
    tile = 128
    row_spec = pl.BlockSpec((tile, hidden), lambda i: (i, 0))
    return pl.pallas_call(
        functools.partial(epilogue_kernel, nz, nx),
        grid=(rows // tile,),
        in_specs=[
            pl.BlockSpec((nz, nx, tile, units), lambda i: (0, 0, i, 0)),
            pl.BlockSpec((nz, nx, 8, units), lambda i: (0, 0, 0, 0)),
            row_spec,
            row_spec,
            pl.BlockSpec((hidden, rank), lambda i: (0, 0)),
        ],
        out_specs=(row_spec, row_spec, pl.BlockSpec((3, tile, rank), lambda i: (0, i, 0))),
        out_shape=(
            jax.ShapeDtypeStruct((rows, hidden), jnp.bfloat16),
            jax.ShapeDtypeStruct((rows, hidden), jnp.bfloat16),
            jax.ShapeDtypeStruct((3, rows, rank), jnp.float32),
        ),
        compiler_params=pltpu.CompilerParams(vmem_limit_bytes=48 * 2**20),
        name="epilogue",
    )(q, sc, gate_pre, up_pre, proj_hidden)


def pair_features(weight, left, right):
    rows, slots = weight.shape
    width = left.shape[1]
    spread = (weight[:, :, None] * left[:, None, :]).reshape(rows, slots * width)
    mats = lax.dot_general(
        spread,
        right,
        (((0,), (0,)), ((), ())),
        precision=lax.Precision.HIGHEST,
        preferred_element_type=jnp.float32,
    )
    return mats.reshape(slots, width * width)


def on_device(
    sizes, activations, out_grad, gate_pre, up_pre, down_weight, proj_model, proj_hidden, lengths
):
    rows_here, width_here = activations.shape
    offsets = jnp.cumsum(lengths) - lengths
    rows = jnp.arange(rows_here, dtype=jnp.int32)[:, None]
    member = jnp.logical_and(rows >= offsets[None, :], rows < (offsets + lengths)[None, :]).astype(
        jnp.float32
    )
    live = jnp.sum(member, axis=1)
    masked_part = out_grad * live[:, None].astype(jnp.bfloat16)
    proj_here = lax.dynamic_slice_in_dim(
        proj_model, lax.axis_index("tensor") * width_here, width_here, axis=0
    )
    early = jnp.concatenate(
        [
            jnp.dot(activations, proj_here, preferred_element_type=jnp.float32),
            jnp.dot(masked_part, proj_here, preferred_element_type=jnp.float32),
        ],
        axis=1,
    )
    early = lax.psum(early, "tensor")
    q, sc = hidden_grads(sizes, masked_part, down_weight)
    grad_gate, grad_up, parts = epilogue(sizes, q, sc, gate_pre, up_pre, proj_hidden)
    rank = proj_hidden.shape[1]
    in_proj, out_proj = early[:, :rank], early[:, rank:]
    weight = member / jnp.sqrt(lengths.astype(jnp.float32))[None, :]
    features = jnp.stack(
        [
            pair_features(weight, in_proj, parts[0]),
            pair_features(weight, in_proj, parts[1]),
            pair_features(weight, parts[2], out_proj),
        ],
        axis=1,
    )
    return (grad_gate, grad_up, lax.psum(features, "tensor"))


def solution(mesh):
    return jax.shard_map(
        functools.partial(on_device, plan(mesh)),
        mesh=mesh,
        in_specs=(
            P("dp", "tensor"),
            P("dp", "tensor"),
            P("dp", "tensor"),
            P("dp", "tensor"),
            P(("tensor", "dp"), None),
            P(),
            P("tensor", None),
            P("dp"),
        ),
        out_specs=(P("dp", "tensor"), P("dp", "tensor"), P("dp", None, None)),
        check_vma=False,
    )
```

```python
import functools

import jax
import jax.numpy as jnp
from jax import lax
from jax.experimental import pallas as pl
from jax.experimental.pallas import tpu as pltpu
from jax.sharding import PartitionSpec as P

MESH = pl.DeviceIdType.MESH
LEVELS = 32767.0


def plan(mesh):
    n_dp, n_tensor = mesh.shape["dp"], mesh.shape["tensor"]
    nz = 4 if n_dp % 4 == 0 else n_dp
    nc = 2 if n_tensor % 2 == 0 else 1
    return nz, n_dp // nz, n_tensor // nc, nc


def grad_kernel(
    nz, nx, ny, nc, tok_in, w_in, q_out, sc_out,
    tok, w, qs, scs,
    loc, zs, zr, ys, yr, cs, cr, xs, xr, rs, rr, ss, sr,
):
    dp = lax.axis_index("dp")
    tn = lax.axis_index("tensor")
    z, x = lax.div(dp, nx), lax.rem(dp, nx)
    y, c = lax.div(tn, nc), lax.rem(tn, nc)
    width = tok.shape[3]
    n_t = ny * nc

    def at_z(zz):
        return (zz * nx + x, tn)

    def at_x(k):
        return (z * nx + lax.rem(x + k, nx), tn)

    def at_y(k):
        return (dp, lax.rem(y + k, ny) * nc + c)

    def at_c(k):
        return (dp, y * nc + lax.rem(c + k, nc))

    barrier = pltpu.get_barrier_semaphore()
    peers = [at_z(lax.rem(z + k, nz)) for k in range(1, nz)]
    peers += [at_x(k) for k in range(1, nx)]
    peers += [at_y(k) for k in range(1, ny)]
    peers += [at_c(k) for k in range(1, nc)]
    own_tok = pltpu.make_async_copy(tok_in, tok.at[z, tn], loc.at[0])
    own_tok.start()
    own_w = pltpu.make_async_copy(w_in, w.at[x], loc.at[1])
    own_w.start()
    for peer in peers:
        pl.semaphore_signal(barrier, inc=1, device_id=peer, device_id_type=MESH)
    pl.semaphore_wait(barrier, len(peers))

    def remote(src, dst, send, recv, device):
        return pltpu.make_async_remote_copy(
            src_ref=src, dst_ref=dst, send_sem=send, recv_sem=recv,
            device_id=device, device_id_type=MESH,
        )

    def w_copy(k):
        return remote(w_in, w.at[x], xs.at[k - 1], xr.at[x], at_x(k))

    def z_copy(b, side):
        target = z + 1 if side else z - 1
        return remote(tok.at[b, tn], tok.at[b, tn], zs.at[b, side], zr.at[b], at_z(target))

    def y_copy(b, k):
        return remote(tok.at[b, tn], tok.at[b, tn], ys.at[b, k - 1], yr.at[b, k - 1], at_y(k))

    def c_copy(b, k, kc):
        t = lax.rem(y - k + ny, ny) * nc + c
        return remote(tok.at[b, t], tok.at[b, t], cs.at[b, k, kc - 1], cr.at[b, k, kc - 1], at_c(kc))

    def q_copy(b, xi):
        return remote(qs.at[b, xi], q_out.at[z, xi], rs.at[b, xi], rr.at[z, xi], at_z(b))

    def sc_copy(b, xi):
        return remote(scs.at[b, xi], sc_out.at[z, xi], ss.at[b, xi], sr.at[z, xi], at_z(b))

    def q_own(xi):
        return pltpu.make_async_copy(qs.at[z, xi], q_out.at[z, xi], rs.at[z, xi])

    def sc_own(xi):
        return pltpu.make_async_copy(scs.at[z, xi], sc_out.at[z, xi], ss.at[z, xi])

    near = jnp.minimum(z, nz - 1 - z)

    def block_of(i):
        half = lax.div(i + 1, 2)
        both = jnp.where(lax.rem(i, 2) == 1, z - half, z + half)
        tail = jnp.where(z == near, i, nz - 1 - i)
        return jnp.where(i <= 2 * near, both, tail)

    def goes_right(b):
        return jnp.logical_and(b <= z, z < nz - 1)

    def goes_left(b):
        return jnp.logical_and(b >= z, z > 0)

    def spread(b):
        pl.when(goes_right(b))(lambda: z_copy(b, 1).start())
        pl.when(goes_left(b))(lambda: z_copy(b, 0).start())
        for k in range(1, ny):
            y_copy(b, k).start()
        for kc in range(1, nc):
            c_copy(b, 0, kc).start()

    def complete(b):
        for k in range(1, ny):
            y_copy(b, k).wait_recv()
            for kc in range(1, nc):
                c_copy(b, k, kc).start()
        for k in range(ny):
            for kc in range(1, nc):
                c_copy(b, k, kc).wait_recv()

    def product(b, xi):
        total = None
        for t in range(n_t):
            part = lax.dot_general(
                tok[b, t], w[xi, :, t * width:(t + 1) * width],
                (((1,), (1,)), ((), ())), preferred_element_type=jnp.float32,
            )
            total = part if total is None else total + part
        top = jnp.maximum(jnp.max(jnp.abs(total), axis=0, keepdims=True), 1e-30)
        qs[b, xi] = jnp.round(total * (LEVELS / top)).astype(jnp.int32).astype(jnp.int16)
        scs[b, xi] = jnp.broadcast_to(top * (1.0 / LEVELS), scs.shape[2:])

        @pl.when(b == z)
        def _():
            q_own(xi).start()
            sc_own(xi).start()

        @pl.when(b != z)
        def _():
            q_copy(b, xi).start()
            sc_copy(b, xi).start()

    own_tok.wait()
    spread(z)
    for k in range(1, nx):
        w_copy(k).start()
    own_w.wait()

    @pl.loop(1, nz + 1)
    def _(i):
        @pl.when(i < nz)
        def _():
            b = block_of(i)
            z_copy(b, 0).wait_recv()
            spread(b)

        b = block_of(i - 1)
        complete(b)
        product(b, x)

    for k in range(1, nx):
        xi = lax.rem(x - k + nx, nx)
        remote(w_in, w.at[xi], xs.at[k - 1], xr.at[xi], at_x(k)).wait_recv()

        @pl.loop(0, nz)
        def _(i):
            product(block_of(lax.rem(i + 1, nz)), xi)

    for k in range(1, nx):
        w_copy(k).wait_send()

    @pl.loop(0, nz)
    def _(b):
        pl.when(goes_right(b))(lambda: z_copy(b, 1).wait_send())
        pl.when(goes_left(b))(lambda: z_copy(b, 0).wait_send())
        for k in range(1, ny):
            y_copy(b, k).wait_send()
        for k in range(ny):
            for kc in range(1, nc):
                c_copy(b, k, kc).wait_send()
        for xi in range(nx):
            @pl.when(b == z)
            def _():
                q_own(xi).wait()
                sc_own(xi).wait()

            @pl.when(b != z)
            def _():
                q_copy(b, xi).wait_send()
                sc_copy(b, xi).wait_send()
                remote(qs.at[b, xi], q_out.at[b, xi], rs.at[b, xi], rr.at[b, xi], at_z(b)).wait_recv()
                remote(scs.at[b, xi], sc_out.at[b, xi], ss.at[b, xi], sr.at[b, xi], at_z(b)).wait_recv()


def hidden_grads(sizes, masked_part, down_weight):
    nz, nx, ny, nc = sizes
    rows, width = masked_part.shape
    units, model = down_weight.shape
    n_t = ny * nc
    dma = pltpu.SemaphoreType.DMA
    any_spec = pl.BlockSpec(memory_space=pl.ANY)
    return pl.pallas_call(
        functools.partial(grad_kernel, nz, nx, ny, nc),
        out_shape=(
            jax.ShapeDtypeStruct((nz, nx, rows, units), jnp.int16),
            jax.ShapeDtypeStruct((nz, nx, 8, units), jnp.float32),
        ),
        in_specs=[any_spec, any_spec],
        out_specs=(any_spec, any_spec),
        scratch_shapes=[
            pltpu.VMEM((nz, n_t, rows, width), jnp.bfloat16),
            pltpu.VMEM((nx, units, model), jnp.bfloat16),
            pltpu.VMEM((nz, nx, rows, units), jnp.int16),
            pltpu.VMEM((nz, nx, 8, units), jnp.float32),
            dma((2,)),
            dma((nz, 2)), dma((nz,)),
            dma((nz, max(ny - 1, 1))), dma((nz, max(ny - 1, 1))),
            dma((nz, ny, max(nc - 1, 1))), dma((nz, ny, max(nc - 1, 1))),
            dma((max(nx - 1, 1),)), dma((nx,)),
            dma((nz, nx)), dma((nz, nx)),
            dma((nz, nx)), dma((nz, nx)),
        ],
        compiler_params=pltpu.CompilerParams(
            collective_id=0, has_side_effects=True, vmem_limit_bytes=56 * 2**20
        ),
        cost_estimate=pl.CostEstimate(
            flops=2 * nz * rows * nx * units * model,
            bytes_accessed=2 * (rows * width + units * model + nz * nx * rows * units),
            transcendentals=0,
        ),
        name="hidden_grads",
    )(masked_part, down_weight)


def epilogue_kernel(nz, nx, q_ref, sc_ref, gate_ref, up_ref, proj_ref, gg_ref, gu_ref, part_ref):
    rows = gate_ref.shape[0]
    units = q_ref.shape[3]
    chunk = nx * units
    total = None
    for zz in range(nz):
        cols = slice(zz * chunk, (zz + 1) * chunk)
        grad = jnp.concatenate(
            [
                q_ref[zz, xi].astype(jnp.int32).astype(jnp.float32) * sc_ref[zz, xi, 0:1, :]
                for xi in range(nx)
            ],
            axis=1,
        )
        gate32 = gate_ref[:, cols].astype(jnp.float32)
        up32 = up_ref[:, cols].astype(jnp.float32)
        sig = jax.nn.sigmoid(gate32)
        silu = gate32 * sig
        gu = (grad * silu).astype(jnp.bfloat16)
        gg = (grad * up32 * sig * (1.0 + gate32 * (1.0 - sig))).astype(jnp.bfloat16)
        hid = (silu * up32).astype(jnp.bfloat16)
        gu_ref[:, cols] = gu
        gg_ref[:, cols] = gg
        stacked = jnp.concatenate([gg, gu, hid], axis=0)
        part = jnp.dot(stacked, proj_ref[cols, :], preferred_element_type=jnp.float32)
        total = part if total is None else total + part
    for i in range(3):
        part_ref[i] = total[i * rows:(i + 1) * rows]


def epilogue(sizes, q, sc, gate_pre, up_pre, proj_hidden):
    nz, nx = sizes[:2]
    rows, hidden = gate_pre.shape
    units, rank = q.shape[3], proj_hidden.shape[1]
    tile = 128
    row_spec = pl.BlockSpec((tile, hidden), lambda i: (i, 0))
    return pl.pallas_call(
        functools.partial(epilogue_kernel, nz, nx),
        grid=(rows // tile,),
        in_specs=[
            pl.BlockSpec((nz, nx, tile, units), lambda i: (0, 0, i, 0)),
            pl.BlockSpec((nz, nx, 8, units), lambda i: (0, 0, 0, 0)),
            row_spec,
            row_spec,
            pl.BlockSpec((hidden, rank), lambda i: (0, 0)),
        ],
        out_specs=(row_spec, row_spec, pl.BlockSpec((3, tile, rank), lambda i: (0, i, 0))),
        out_shape=(
            jax.ShapeDtypeStruct((rows, hidden), jnp.bfloat16),
            jax.ShapeDtypeStruct((rows, hidden), jnp.bfloat16),
            jax.ShapeDtypeStruct((3, rows, rank), jnp.float32),
        ),
        compiler_params=pltpu.CompilerParams(vmem_limit_bytes=48 * 2**20),
        name="epilogue",
    )(q, sc, gate_pre, up_pre, proj_hidden)


def pair_features(weight, left, right):
    rows, slots = weight.shape
    width = left.shape[1]
    spread = (weight[:, :, None] * left[:, None, :]).reshape(rows, slots * width)
    mats = lax.dot_general(
        spread,
        right,
        (((0,), (0,)), ((), ())),
        precision=lax.Precision.HIGHEST,
        preferred_element_type=jnp.float32,
    )
    return mats.reshape(slots, width * width)


def sum_over_tensor(value, n_tensor):
    if n_tensor & (n_tensor - 1):
        return lax.psum(value, "tensor")
    step = 1
    while step < n_tensor:
        pairs = [(i, i ^ step) for i in range(n_tensor)]
        value = value + lax.ppermute(value, "tensor", pairs)
        step *= 2
    return value


def on_device(
    sizes, activations, out_grad, gate_pre, up_pre, down_weight, proj_model, proj_hidden, lengths
):
    rows_here, width_here = activations.shape
    offsets = jnp.cumsum(lengths) - lengths
    rows = jnp.arange(rows_here, dtype=jnp.int32)[:, None]
    member = jnp.logical_and(rows >= offsets[None, :], rows < (offsets + lengths)[None, :]).astype(
        jnp.float32
    )
    live = jnp.sum(member, axis=1)
    masked_part = out_grad * live[:, None].astype(jnp.bfloat16)
    proj_here = lax.dynamic_slice_in_dim(
        proj_model, lax.axis_index("tensor") * width_here, width_here, axis=0
    )
    early = jnp.concatenate(
        [
            jnp.dot(activations, proj_here, preferred_element_type=jnp.float32),
            jnp.dot(masked_part, proj_here, preferred_element_type=jnp.float32),
        ],
        axis=1,
    )
    early = lax.psum(early, "tensor")
    q, sc = hidden_grads(sizes, masked_part, down_weight)
    grad_gate, grad_up, parts = epilogue(sizes, q, sc, gate_pre, up_pre, proj_hidden)
    rank = proj_hidden.shape[1]
    in_proj, out_proj = early[:, :rank], early[:, rank:]
    weight = member / jnp.sqrt(lengths.astype(jnp.float32))[None, :]
    features = jnp.stack(
        [
            pair_features(weight, in_proj, parts[0]),
            pair_features(weight, in_proj, parts[1]),
            pair_features(weight, parts[2], out_proj),
        ],
        axis=1,
    )
    return (grad_gate, grad_up, sum_over_tensor(features, sizes[2] * sizes[3]))


def solution(mesh):
    return jax.shard_map(
        functools.partial(on_device, plan(mesh)),
        mesh=mesh,
        in_specs=(
            P("dp", "tensor"),
            P("dp", "tensor"),
            P("dp", "tensor"),
            P("dp", "tensor"),
            P(("tensor", "dp"), None),
            P(),
            P("tensor", None),
            P("dp"),
        ),
        out_specs=(P("dp", "tensor"), P("dp", "tensor"), P("dp", None, None)),
        check_vma=False,
    )
```
